128 devices in a mesh: fsdp: 32 (over z, y, core), tensor: 4 (over x).
Axes of the slice: x: 4, y: 4, z: 4, core: 2. Of those that a mesh axis runs over, the one named last changes fastest.
Arguments:
- gradient: bfloat16 [4608, 36864], P('fsdp', 'tensor'), may hold values from -8 to 8
- left_basis: bfloat16 [4608, 256], P('fsdp'), may hold values from -6 to 6
- right_basis: bfloat16 [36864, 256], P('tensor'), may hold values from -6 to 6
- left_scale: float32 [256], replicated, may hold values from 2 to 20
- right_scale: float32 [256], replicated, may hold values from 2 to 20
Outputs:
- update: bfloat16 [4608, 36864], P('fsdp', 'tensor')
- left_basis_new: float32 [4608, 256], P('fsdp')
- left_scale_new: float32 [256], replicated
- right_basis_new: float32 [4, 9216, 256], P('tensor', 'fsdp')
- right_scale_new: float32 [256], replicated
The draws below stay inside these ranges and needn't reach their ends.
All inputs are finite; a program needn't handle non-finite values.
Results may differ from the reference program's by a relative error of at most 0.0095.
Values may be sent and summed in bfloat16 or wider, within the bound.
No kernel may reach another device: no remote copies, remote signals or barrier semaphores. Data moves between devices by JAX's collectives and lax.ppermute only.
A program may use at most 128 MiB of HBM per device.

```python
import math
import jax
import jax.numpy as jnp
from jax import lax

D = 4608
FF = 36864
RANK = 256
N_TENSOR = 4


def shared_factors(key):
    left_factor = jax.random.normal(jax.random.fold_in(key, 101), (D, RANK), jnp.float32)
    right_factor = jax.random.normal(jax.random.fold_in(key, 102), (FF, RANK), jnp.float32)
    return (left_factor, right_factor)


def structured_field(left_factor, right_factor, key_scale, top_scale, noise_part):
    strengths = jnp.exp(jax.random.uniform(key_scale, (RANK,), jnp.float32, 0.0, math.log(top_scale)))
    mean_square = (top_scale * top_scale - 1.0) / (2.0 * math.log(top_scale))
    weights = strengths * (1.0 / math.sqrt(RANK * mean_square))
    low_part = jnp.dot(left_factor * weights, right_factor.T, precision=lax.Precision.HIGHEST)
    return jnp.clip(low_part + noise_part, -8.0, 8.0).astype(jnp.bfloat16)


def mixed_basis(factor, noise_part, alignment):
    rest = math.sqrt(1.0 - alignment * alignment)
    return jnp.clip(alignment * factor + rest * noise_part, -6.0, 6.0).astype(jnp.bfloat16)


def draw_gradient(key, part):
    left_factor, right_factor = shared_factors(key)
    key = jax.random.fold_in(key, 1)
    key_scale, key_noise = jax.random.split(key)
    top_scale = 10.0
    noise_part = 0.3 * jax.random.normal(key_noise, (D, FF), jnp.float32)
    return structured_field(left_factor, right_factor, key_scale, top_scale, noise_part)


def draw_left_basis(key, part):
    left_factor, right_factor = shared_factors(key)
    key = jax.random.fold_in(key, 2)
    alignment = 0.85
    noise_part = jax.random.normal(key, (D, RANK), jnp.float32)
    return mixed_basis(left_factor, noise_part, alignment)


def draw_right_basis(key, part):
    left_factor, right_factor = shared_factors(key)
    key = jax.random.fold_in(key, 3)
    alignment = 0.85
    noise_part = jax.random.normal(key, (FF, RANK), jnp.float32)
    return mixed_basis(right_factor, noise_part, alignment)


def setup_inputs(seed: int = 0) -> dict:
    key_list = jax.random.split(jax.random.key(seed), 6)
    gradient = draw_gradient(jax.random.fold_in(key_list[5], 71), 0)
    left_basis = draw_left_basis(jax.random.fold_in(key_list[5], 71), 0)
    right_basis = draw_right_basis(jax.random.fold_in(key_list[5], 71), 0)
    left_scale = jnp.clip(jnp.exp(jax.random.uniform(key_list[3], (RANK,), jnp.float32, math.log(2.0), math.log(20.0))), 2.0, 20.0)
    right_scale = jnp.clip(jnp.exp(jax.random.uniform(key_list[4], (RANK,), jnp.float32, math.log(2.0), math.log(20.0))), 2.0, 20.0)
    return {"gradient": gradient, "left_basis": left_basis, "right_basis": right_basis, "left_scale": left_scale, "right_scale": right_scale}


decay_rate = 0.9

def tall_product(first, second):
    return lax.dot_general(first.astype(jnp.float32), second.astype(jnp.float32), (((0,), (0,)), ((), ())), preferred_element_type=jnp.float32)

def cholesky_basis(rows, count):
    gram = jnp.dot(rows.T.astype(jnp.float32), rows.astype(jnp.float32), precision=lax.Precision.HIGHEST, preferred_element_type=jnp.float32) / count
    lower = jnp.linalg.cholesky(gram)
    basis = lax.linalg.triangular_solve(lower, rows, left_side=False, lower=True, transpose_a=True)
    return (basis, jnp.diagonal(lower))

def reference(gradient, left_basis, right_basis, left_scale, right_scale):
    left_proj = tall_product(gradient, left_basis).astype(jnp.bfloat16)
    left_rows = decay_rate * left_basis.astype(jnp.float32) * left_scale + jnp.dot(gradient.astype(jnp.float32), left_proj.astype(jnp.float32), preferred_element_type=jnp.float32) / FF
    right_image = jnp.dot(gradient.astype(jnp.float32), right_basis.astype(jnp.float32), preferred_element_type=jnp.float32).astype(jnp.bfloat16)
    right_rows = decay_rate * right_basis.astype(jnp.float32) * right_scale + tall_product(gradient, right_image) / D
    left_new, left_scale_new = cholesky_basis(left_rows, D)
    right_new, right_scale_new = cholesky_basis(right_rows, FF)
    left_damp = (left_scale_new + 1.0) ** (-0.5) - 1.0
    right_damp = (right_scale_new + 1.0) ** (-0.5) - 1.0
    left_cast = left_new.astype(jnp.bfloat16)
    right_cast = right_new.astype(jnp.bfloat16)
    right_coeff = (jnp.dot(gradient.astype(jnp.float32), right_cast.astype(jnp.float32), preferred_element_type=jnp.float32) * (right_damp / FF)).astype(jnp.bfloat16)
    mixed = gradient.astype(jnp.float32) + lax.dot_general(right_coeff.astype(jnp.float32), right_cast.astype(jnp.float32), (((1,), (1,)), ((), ())), preferred_element_type=jnp.float32)
    mixed_cast = mixed.astype(jnp.bfloat16)
    left_coeff = (tall_product(mixed_cast, left_cast) * (left_damp / D)).astype(jnp.bfloat16)
    update = mixed + lax.dot_general(left_cast.astype(jnp.float32), left_coeff.astype(jnp.float32), (((1,), (1,)), ((), ())), preferred_element_type=jnp.float32)
    right_blocks = right_new.reshape(N_TENSOR, FF // N_TENSOR, RANK)
    return (update.astype(jnp.bfloat16), left_new, left_scale_new, right_blocks, right_scale_new)
```

```python
import jax
import jax.numpy as jnp
from jax import lax
from jax.experimental import pallas as pl
from jax.experimental.pallas import tpu as pltpu
from jax.sharding import PartitionSpec as P

D = 4608
FF = 36864
RANK = 256
BLOCK = 64
HIGHEST = lax.Precision.HIGHEST

def eliminate(group_list):
    count = BLOCK // 8
    many = 4
    row_iota = lax.broadcasted_iota(jnp.int32, (8, 2 * BLOCK), 0)
    for j in range(0, BLOCK, many):
        g, s = j // 8, j % 8
        for groups in group_list:
            columns = [
                [jnp.broadcast_to(x[:, j + k : j + k + 1], x.shape) for x in groups[g:]]
                for k in range(many)
            ]
            pivot_rows = [groups[g][s + k : s + k + 1] for k in range(many)]
            inverses = []
            for k in range(many):
                here = columns[k]
                inverse = 1.0 / here[0][s + k : s + k + 1]
                inverses.append(inverse)
                for m in range(k + 1, many):
                    low = columns[m][0][s + k : s + k + 1] * inverse
                    pivot_rows[m] = pivot_rows[m] - low * pivot_rows[k]
                    columns[m] = [x - y * low for x, y in zip(columns[m], here)]
            pivot_rows = [row * inverse for row, inverse in zip(pivot_rows, inverses)]
            for i in range(g, count):
                value = groups[i]
                for k in range(many):
                    part = columns[k][i - g]
                    if i == g:
                        part = jnp.where(row_iota > s + k, part, 0.0)
                    value = value - part * pivot_rows[k]
                groups[i] = value
    return group_list


def factor(works, invs, diags):
    for inv in invs:
        inv[...] = jnp.zeros_like(inv)
    row = lax.broadcasted_iota(jnp.int32, (BLOCK, 2 * BLOCK), 0)
    col = lax.broadcasted_iota(jnp.int32, (BLOCK, 2 * BLOCK), 1)
    unit = jnp.where(col - BLOCK == row, 1.0, 0.0).astype(jnp.float32)
    diag_mask = col == row
    for k in range(0, RANK, BLOCK):
        end = k + BLOCK
        start = []
        for work in works:
            x = jnp.concatenate([work[k:end, k:end], unit[:, BLOCK:]], axis=1)
            start.append([x[i : i + 8] for i in range(0, BLOCK, 8)])
        done = eliminate(start)
        for groups, work, inv, diag in zip(done, works, invs, diags):
            x = jnp.concatenate(groups, axis=0)
            pivots = jnp.sum(jnp.where(diag_mask, x, 0.0), axis=1, keepdims=True)
            x = x * lax.rsqrt(pivots)
            diag[:, k:end] = jnp.sum(jnp.where(diag_mask, x, 0.0), axis=0, keepdims=True)[:, :BLOCK]
            t = x[:, BLOCK:]
            inv[k:end, k:end] = t
            if k:
                inv[k:end, :k] = jnp.dot(t, inv[k:end, :k], precision=HIGHEST, preferred_element_type=jnp.float32)
            if end < RANK:
                u = jnp.dot(t, work[k:end, end:], precision=HIGHEST, preferred_element_type=jnp.float32)
                both = jnp.concatenate([inv[k:end, :end], u], axis=1)
                step = lax.dot_general(u, both, (((0,), (0,)), ((), ())), precision=HIGHEST, preferred_element_type=jnp.float32)
                inv[end:, :end] -= step[:, :end]
                work[end:, end:] -= step[:, end:]


decay_rate = 0.9
ROWS = 144
SHARE = 288
OWN = 36
LINE = 40
FOUR = 4 * LINE
WIDE = 4 * SHARE
PIECE = 16 * LINE
TILES = WIDE // 128
TALL = 328
SIDE = 64 * LINE


def tall_product(first, second):
    return lax.dot_general(
        first, second, (((0,), (0,)), ((), ())), preferred_element_type=jnp.float32
    )


def wide_product(first, second):
    return lax.dot_general(
        first, second, (((1,), (1,)), ((), ())), preferred_element_type=jnp.float32
    )


def times_inverse(rows, inverse):
    return lax.dot_general(
        rows,
        inverse,
        (((1,), (1,)), ((), ())),
        precision=HIGHEST,
        preferred_element_type=jnp.float32,
    )


def whole():
    return pl.BlockSpec(memory_space=pltpu.VMEM)


LIMIT = pltpu.CompilerParams(vmem_limit_bytes=62 * 1024 * 1024)


def stack_tiles(value):
    tiles = [value[:, 128 * k : 128 * (k + 1)] for k in range(TILES)]
    tiles.append(jnp.zeros((TALL - OWN * TILES, 128), jnp.float32))
    return jnp.concatenate(tiles, axis=0).astype(jnp.bfloat16)


def unstack_tiles(value):
    value = value.astype(jnp.float32)
    return jnp.concatenate([value[OWN * k : OWN * (k + 1)] for k in range(TILES)], axis=1)


def pack_kernel(block_ref, out_ref):
    value = block_ref[...].astype(jnp.float32)
    for p in range(8):
        quarters = [
            value[t * OWN : (t + 1) * OWN, p * SHARE : (p + 1) * SHARE] for t in range(4)
        ]
        out_ref[p] = stack_tiles(jnp.concatenate(quarters, axis=1))


def pack(block):
    n_row = FF // 4 // SHARE
    return pl.pallas_call(
        pack_kernel,
        grid=(n_row // 8,),
        in_specs=[pl.BlockSpec((ROWS, 8 * SHARE), lambda i: (0, i))],
        out_specs=pl.BlockSpec((8, TALL, 128), lambda i: (i, 0, 0)),
        out_shape=jax.ShapeDtypeStruct((n_row, TALL, 128), jnp.bfloat16),
        compiler_params=LIMIT,
    )(block)


def unpack_kernel(parcel_ref, out_ref):
    values = [unstack_tiles(parcel_ref[p]) for p in range(8)]
    quarters = [
        jnp.concatenate([value[:, t * SHARE : (t + 1) * SHARE] for value in values], axis=1)
        for t in range(4)
    ]
    out_ref[...] = jnp.concatenate(quarters, axis=0).astype(jnp.bfloat16)


def unpack(parcels):
    n_row = parcels.shape[0]
    return pl.pallas_call(
        unpack_kernel,
        grid=(n_row // 8,),
        in_specs=[pl.BlockSpec((8, TALL, 128), lambda i: (i, 0, 0))],
        out_specs=pl.BlockSpec((ROWS, 8 * SHARE), lambda i: (0, i)),
        out_shape=jax.ShapeDtypeStruct((ROWS, n_row * SHARE), jnp.bfloat16),
        compiler_params=LIMIT,
    )(parcels)


def strip_kernel(where_ref, parcel_ref, own_ref, scale_ref, *refs):
    piece_refs = refs[:10]
    strip_ref, rows_ref, factor_ref, gram_ref, quarter, work = refs[10:]
    step = pl.program_id(0)

    @pl.when(step == 0)
    def _():
        work[...] = jnp.zeros_like(work)

    lines = []
    empty = jnp.zeros((LINE - OWN, WIDE), jnp.float32)
    for p in range(parcel_ref.shape[0]):
        value = jnp.concatenate([unstack_tiles(parcel_ref[p, 0]), empty], axis=0)
        lines += [value[:, t * SHARE : (t + 1) * SHARE] for t in range(4)]
    strip_ref[0] = jnp.concatenate(lines, axis=0).astype(jnp.bfloat16)
    for t in range(4):
        quarter[t] = jnp.concatenate(lines[t::4], axis=0).astype(jnp.bfloat16)

    def add_products(own, right, across, across_next, left):
        opposite = jnp.where(step % 2 == 0, across[...], across_next[...])
        thin = jnp.concatenate([own[...], right[...], opposite, left[...]], axis=0)
        order = [quarter[(where_ref[1] + d) % 4] for d in range(4)]
        work[...] += tall_product(jnp.concatenate(order, axis=0), thin)

    @pl.when(step < 2)
    def _():
        add_products(*piece_refs[:5])

    @pl.when(step >= 2)
    def _():
        add_products(*piece_refs[5:])

    @pl.when(step == pl.num_programs(0) - 1)
    def _():
        right_rows = (
            decay_rate * own_ref[...].astype(jnp.float32) * scale_ref[...] + work[:, RANK:] / D
        )
        rows_ref[...] = right_rows
        factor_ref[:, :RANK] = work[:, :RANK].astype(jnp.bfloat16)
        factor_ref[:, RANK:] = right_rows.astype(jnp.bfloat16)
        gram_ref[...] = (
            lax.dot_general(
                right_rows,
                right_rows,
                (((0,), (0,)), ((), ())),
                precision=HIGHEST,
                preferred_element_type=jnp.float32,
            )
            / FF
        )


def smem():
    return pl.BlockSpec(memory_space=pltpu.SMEM)


def strip_products(where, parcels, own_rows, right_scale, pieces):
    block = 8 * FOUR

    def fixed(shape):
        return pl.BlockSpec(shape, lambda i, where: (0,) * len(shape))

    def by_core(shape):
        return pl.BlockSpec(shape, lambda i, where: (i % 2, (where[0] + i // 2) % 2, 0, 0))

    mine = pl.BlockSpec((8 * LINE, 2 * RANK), lambda i, where: (jnp.minimum(i, 1), 0))
    other = pl.BlockSpec((8 * LINE, 2 * RANK), lambda i, where: (jnp.maximum(i - 2, 0), 0))
    half = fixed((8 * LINE, 2 * RANK))
    return pl.pallas_call(
        strip_kernel,
        grid_spec=pltpu.PrefetchScalarGridSpec(
            num_scalar_prefetch=1,
            grid=(4,),
            in_specs=[
                by_core((8, 1, TALL, 128)),
                fixed((SHARE, RANK)),
                fixed((1, RANK)),
            ]
            + [mine, mine, half, half, mine]
            + [other, other, half, half, other],
            out_specs=(
                pl.BlockSpec((1, block, SHARE), lambda i, where: (i // 2, i % 2, 0)),
                fixed((SHARE, RANK)),
                fixed((SHARE, 2 * RANK)),
                fixed((RANK, RANK)),
            ),
            scratch_shapes=[
                pltpu.VMEM((4, 8 * LINE, SHARE), jnp.bfloat16),
                pltpu.VMEM((SHARE, 2 * RANK), jnp.float32),
            ],
        ),
        out_shape=(
            jax.ShapeDtypeStruct((2, SIDE, SHARE), jnp.bfloat16),
            jax.ShapeDtypeStruct((SHARE, RANK), jnp.float32),
            jax.ShapeDtypeStruct((SHARE, 2 * RANK), jnp.bfloat16),
            jax.ShapeDtypeStruct((RANK, RANK), jnp.float32),
        ),
        compiler_params=LIMIT,
    )(
        where,
        parcels.reshape(16, 2, TALL, 128),
        own_rows,
        right_scale[None],
        *pieces,
    )


def away_kernel(strip_ref, factor_ref, out_ref):
    out_ref[...] = jnp.dot(
        strip_ref[0], factor_ref[...], preferred_element_type=jnp.float32
    ).astype(jnp.bfloat16)


def home_kernel(
    where_ref, strip_ref, factor_ref, other_ref, gram_ref, other_gram_ref, out_ref
):
    step = pl.program_id(0)
    product = jnp.dot(strip_ref[0], factor_ref[...], preferred_element_type=jnp.float32)
    product = product + other_ref[...].astype(jnp.float32)
    rows = pl.ds(pl.multiple_of(where_ref[0] * 128 + step * 32, 32), 32)
    gram = gram_ref[rows] + other_gram_ref[rows]
    high = gram.astype(jnp.bfloat16)
    low = (gram - high.astype(jnp.float32)).astype(jnp.bfloat16)
    to = lax.broadcasted_iota(jnp.int32, (8 * 16, 32), 0)
    source = lax.broadcasted_iota(jnp.int32, (8 * 16, 32), 1)
    spare = to % 8 - (OWN - 32)
    pick = jnp.where(
        (to // 8 * 2 + spare == source) & (spare >= 0) & (spare < 2), 1.0, 0.0
    ).astype(jnp.bfloat16)
    tail = jnp.concatenate(
        [
            jnp.dot(pick, high, preferred_element_type=jnp.float32),
            jnp.dot(pick, low, preferred_element_type=jnp.float32),
        ],
        axis=1,
    )
    lines = []
    for c in range(16):
        line = product[c * LINE : (c + 1) * LINE]
        lines += [line[:32], line[32:] + tail[c * 8 : (c + 1) * 8]]
    out_ref[...] = jnp.concatenate(lines, axis=0).astype(jnp.bfloat16)


def away_sums(strip, factors):
    return pl.pallas_call(
        away_kernel,
        grid=(4,),
        in_specs=[
            pl.BlockSpec((1, PIECE, SHARE), lambda i: (1, i, 0)),
            pl.BlockSpec((SHARE, 2 * RANK), lambda i: (0, 0)),
        ],
        out_specs=pl.BlockSpec((PIECE, 2 * RANK), lambda i: (i, 0)),
        out_shape=jax.ShapeDtypeStruct((SIDE, 2 * RANK), jnp.bfloat16),
        compiler_params=LIMIT,
    )(strip, factors)


def home_sums(where, strip, factors, other, gram, other_gram):
    sums = pl.pallas_call(
        home_kernel,
        grid_spec=pltpu.PrefetchScalarGridSpec(
            num_scalar_prefetch=1,
            grid=(4,),
            in_specs=[
                pl.BlockSpec((1, PIECE, SHARE), lambda i, where: (0, i, 0)),
                pl.BlockSpec((SHARE, 2 * RANK), lambda i, where: (0, 0)),
                pl.BlockSpec((PIECE, 2 * RANK), lambda i, where: (i, 0)),
                pl.BlockSpec((RANK, RANK), lambda i, where: (0, 0)),
                pl.BlockSpec((RANK, RANK), lambda i, where: (0, 0)),
            ],
            out_specs=pl.BlockSpec((PIECE, 2 * RANK), lambda i, where: (i, 0)),
        ),
        out_shape=jax.ShapeDtypeStruct((SIDE, 2 * RANK), jnp.bfloat16),
        compiler_params=LIMIT,
    )(where, strip, factors, other, gram, other_gram)
    return sums.reshape(64, LINE, 2 * RANK)


def lines_kernel(sums_ref, basis_ref, scale_ref, rows_ref, lines_ref, work):
    step = pl.program_id(0)

    @pl.when(step == 0)
    def _():
        work[...] = jnp.zeros_like(work)

    total = work[...]
    for c in range(sums_ref.shape[0]):
        total += sums_ref[c].astype(jnp.float32)
    work[...] = total

    @pl.when(step == pl.num_programs(0) - 1)
    def _():
        left = work[:, :RANK]
        rows = decay_rate * basis_ref[...].astype(jnp.float32) * scale_ref[...] + left / FF
        rows_ref[:, :RANK] = rows
        rows_ref[:, RANK:] = work[:, RANK:]
        gram = left[32:] + work[32:, RANK:]
        high = gram.astype(jnp.bfloat16).astype(jnp.float32)
        low = pltpu.roll(gram - high, 2, 0)
        place = lax.broadcasted_iota(jnp.int32, (8, RANK), 0)
        last = jnp.where(
            place < OWN - 32, rows[32:], jnp.where(place < OWN - 30, high, low)
        )
        line = jnp.concatenate([rows[:32], last], axis=0).astype(jnp.bfloat16)
        lines_ref[...] = jnp.broadcast_to(line[None], lines_ref.shape)


def own_lines(sums, basis, scale):
    per = 16

    def fixed(shape):
        return pl.BlockSpec(shape, lambda i: (0,) * len(shape))

    return pl.pallas_call(
        lines_kernel,
        grid=(sums.shape[0] // per,),
        in_specs=[
            pl.BlockSpec((per, LINE, 2 * RANK), lambda i: (i, 0, 0)),
            fixed((LINE, RANK)),
            fixed((1, RANK)),
        ],
        out_specs=(fixed((LINE, 2 * RANK)), fixed((64, LINE, RANK))),
        out_shape=(
            jax.ShapeDtypeStruct((LINE, 2 * RANK), jnp.float32),
            jax.ShapeDtypeStruct((64, LINE, RANK), jnp.bfloat16),
        ),
        scratch_shapes=[pltpu.VMEM((LINE, 2 * RANK), jnp.float32)],
        compiler_params=LIMIT,
    )(sums, basis, scale[None])


def read_side(lines_ref, left_ref, gram, store):
    valid = lax.broadcasted_iota(jnp.int32, (PIECE, RANK), 0) % LINE < OWN
    to = lax.broadcasted_iota(jnp.int32, (32, PIECE), 0)
    source = lax.broadcasted_iota(jnp.int32, (32, PIECE), 1) - (to // 2 * LINE + OWN + to % 2)
    pick = jnp.where((source == 0) | (source == 2), 1.0, 0.0).astype(jnp.bfloat16)
    gram[...] = jnp.zeros_like(gram)
    for i in range(SIDE // PIECE):
        value = lines_ref[i * PIECE : (i + 1) * PIECE]
        store(i * 32, jnp.dot(pick, value, preferred_element_type=jnp.float32))
        value = jnp.where(valid, value.astype(jnp.float32), 0.0).astype(jnp.bfloat16)
        left_ref[i * PIECE : (i + 1) * PIECE] = value
        gram[...] += tall_product(value, value)


def side_kernel(lines_ref, left_ref, gram_ref, rows_ref):
    def store(spot, value):
        rows_ref[spot : spot + 32] = value

    read_side(lines_ref, left_ref, gram_ref, store)


def own_side(lines):
    return pl.pallas_call(
        side_kernel,
        in_specs=[whole()],
        out_specs=(whole(),) * 3,
        out_shape=(
            jax.ShapeDtypeStruct((SIDE, RANK), jnp.bfloat16),
            jax.ShapeDtypeStruct((RANK, RANK), jnp.float32),
            jax.ShapeDtypeStruct((128, RANK), jnp.float32),
        ),
        compiler_params=LIMIT,
    )(lines)


def factor_kernel(
    where_ref, gram_ref, rows_ref, other_ref, sums_ref, left_ref, coeff_ref, left_inv, right_inv,
    left_diag, right_diag, left_work, right_work,
):
    core = where_ref[0]

    def store(spot, value):
        right_work[pl.ds(pl.multiple_of((1 - core) * 128 + spot, 32), 32)] = value

    read_side(other_ref, left_ref, left_work, store)
    right_work[pl.ds(pl.multiple_of(core * 128, 128), 128)] = rows_ref[...]
    left_work[...] = (gram_ref[...] + left_work[...]) / D
    factor((left_work, right_work), (left_inv, right_inv), (left_diag, right_diag))
    damp = lax.rsqrt(right_diag[...] + 1.0) - 1.0
    coeff = times_inverse(sums_ref[:, RANK:], right_inv[...]) * (damp / FF)
    keep = lax.broadcasted_iota(jnp.int32, (LINE, RANK), 0) < OWN
    coeff = jnp.where(keep, coeff, 0.0).astype(jnp.bfloat16)
    coeff_ref[...] = jnp.broadcast_to(coeff[None], coeff_ref.shape)


def factor_grams(where, gram, rows, other, sums):
    square = jax.ShapeDtypeStruct((RANK, RANK), jnp.float32)
    line = jax.ShapeDtypeStruct((1, RANK), jnp.float32)
    return pl.pallas_call(
        factor_kernel,
        in_specs=[smem()] + [whole()] * 4,
        out_specs=(whole(),) * 6,
        out_shape=(
            jax.ShapeDtypeStruct((SIDE, RANK), jnp.bfloat16),
            jax.ShapeDtypeStruct((64, LINE, RANK), jnp.bfloat16),
            square,
            square,
            line,
            line,
        ),
        scratch_shapes=[pltpu.VMEM((RANK, RANK), jnp.float32)] * 2,
        compiler_params=LIMIT,
    )(where, gram, rows, other, sums)


def mix(strip, coeff, new, left, work):
    value = strip.astype(jnp.float32) + wide_product(coeff, new.astype(jnp.bfloat16))
    work[...] += tall_product(value.astype(jnp.bfloat16), left)
    return value


def mixed_kernel(strip_ref, coeff_ref, left_ref, new_ref, mixed_ref, work_ref):
    @pl.when(pl.program_id(0) == 0)
    def _():
        work_ref[...] = jnp.zeros_like(work_ref)

    mixed_ref[...] = mix(strip_ref[0], coeff_ref[...], new_ref[...], left_ref[...], work_ref)


def own_mixed(strip, mine, left_mine, right_new):
    block = 8 * FOUR
    part = pl.BlockSpec((block, RANK), lambda i: (i, 0))
    fixed = pl.BlockSpec((SHARE, RANK), lambda i: (0, 0))
    return pl.pallas_call(
        mixed_kernel,
        grid=(2,),
        in_specs=[pl.BlockSpec((1, block, SHARE), lambda i: (0, i, 0)), part, part, fixed],
        out_specs=(pl.BlockSpec((block, SHARE), lambda i: (i, 0)), fixed),
        out_shape=(
            jax.ShapeDtypeStruct((SIDE, SHARE), jnp.float32),
            jax.ShapeDtypeStruct((SHARE, RANK), jnp.float32),
        ),
        compiler_params=LIMIT,
    )(strip, mine, left_mine, right_new)


def update_kernel(
    where_ref, strip_ref, coeff_ref, mixed_ref, work_ref, left_mine, left_other, new_ref,
    damp_ref, out_ref, mixed, work, left_coeff,
):
    step = pl.program_id(0)
    block = strip_ref.shape[1]

    def spot(index):
        return pl.ds(pl.multiple_of(index * block, block), block)

    @pl.when(step == 0)
    def _():
        work[...] = work_ref[...]

    @pl.when(step < 2)
    def _():
        mixed[spot(step)] = mix(
            strip_ref[0], coeff_ref[...], new_ref[...], left_other[spot(step)], work
        )

    @pl.when(step == 2)
    def _():
        left_coeff[...] = (work[...] * (damp_ref[...] / D)).astype(jnp.bfloat16)

    def write(value, left):
        value = value + wide_product(left, left_coeff[...])
        for p in range(block // FOUR):
            quarters = [
                value[p * FOUR + t * LINE : p * FOUR + t * LINE + OWN] for t in range(4)
            ]
            out_ref[p, 0] = stack_tiles(jnp.concatenate(quarters, axis=1))

    @pl.when((step >= 2) & (step < 4))
    def _():
        write(mixed_ref[...], left_mine[spot(step - 2)])

    @pl.when(step >= 4)
    def _():
        write(mixed[spot(step - 4)], left_other[spot(step - 4)])


def update_parcels(where, strip, other, mixed, work, left_mine, left_other, right_new, left_damp):
    block = 8 * FOUR

    def fixed(shape):
        return pl.BlockSpec(shape, lambda i, where: (0,) * len(shape))

    def out_block(i, where):
        place = jnp.maximum(i - 2, 0)
        return (place % 2, (where[0] + place // 2) % 2, 0, 0)

    parcels = pl.pallas_call(
        update_kernel,
        grid_spec=pltpu.PrefetchScalarGridSpec(
            num_scalar_prefetch=1,
            grid=(6,),
            in_specs=[
                pl.BlockSpec((1, block, SHARE), lambda i, where: (1, jnp.minimum(i, 1), 0)),
                pl.BlockSpec((block, RANK), lambda i, where: (jnp.minimum(i, 1), 0)),
                pl.BlockSpec((block, SHARE), lambda i, where: (jnp.clip(i - 2, 0, 1), 0)),
                fixed((SHARE, RANK)),
                fixed((SIDE, RANK)),
                fixed((SIDE, RANK)),
                fixed((SHARE, RANK)),
                fixed((1, RANK)),
            ],
            out_specs=pl.BlockSpec((8, 1, TALL, 128), out_block),
            scratch_shapes=[
                pltpu.VMEM((SIDE, SHARE), jnp.float32),
                pltpu.VMEM((SHARE, RANK), jnp.float32),
                pltpu.VMEM((SHARE, RANK), jnp.bfloat16),
            ],
        ),
        out_shape=jax.ShapeDtypeStruct((16, 2, TALL, 128), jnp.bfloat16),
        compiler_params=LIMIT,
    )(where, strip, other, mixed, work, left_mine, left_other, right_new, left_damp[None])
    return parcels.reshape(32, TALL, 128)


def ring(value, axis):
    found = [value]
    for step in (3, 2, 1):
        found.append(lax.ppermute(value, axis, [(i, (i + step) % 4) for i in range(4)]))
    return found


def swap(value):
    return lax.ppermute(value, "core", [(0, 1), (1, 0)])


def shift(value, step):
    return lax.ppermute(value, "tensor", [(i, (i + step) % 4) for i in range(4)])


def gather_rest(lines):
    left, right = shift(lines, 1), shift(lines, -1)
    half = lines.shape[0] // 2
    mine = [lines, right, shift(left[:half], 1), shift(right[half:], -1), left]
    return mine + [swap(piece) for piece in mine]


def gather_sets(copies, beside=()):
    mine = lax.all_to_all(copies, ("z", "y", "tensor"), 0, 0)
    mine = mine.reshape(SIDE, mine.shape[2])
    mine, beside = lax.optimization_barrier((mine, beside))
    return mine, swap(mine), beside


def image_kernel(spot_ref, basis_ref, first, second, third, fourth, out_ref):
    spot = spot_ref[0]
    image = (first[spot] + second[spot]) + (third[spot] + fourth[spot])
    line = jnp.concatenate([basis_ref[...], image.astype(jnp.bfloat16)], axis=1)
    out_ref[...] = jnp.broadcast_to(line[None], out_ref.shape)


def image_lines(basis, image, packed):
    spot = jnp.reshape(lax.axis_index("tensor"), (1,)).astype(jnp.int32)
    found, packed = lax.optimization_barrier((ring(image, "tensor"), packed))
    copies = pl.pallas_call(
        image_kernel,
        in_specs=[smem()] + [whole()] * 5,
        out_specs=whole(),
        out_shape=jax.ShapeDtypeStruct((16, LINE, 2 * RANK), jnp.bfloat16),
    )(spot, basis, *found)
    lines = lax.all_to_all(copies, ("z", "y"), 0, 0)
    return lines.reshape(PIECE, 2 * RANK), packed


def in_lines(rows):
    return jnp.pad(rows.reshape(4, OWN, RANK), ((0, 0), (0, LINE - OWN), (0, 0)))


def shards(gradient, left_basis, right_basis, left_scale, right_scale):
    t_place = lax.axis_index("tensor")
    place = (lax.axis_index("z") * 4 + lax.axis_index("y")) * 2 + lax.axis_index("core")
    where = jnp.stack([lax.axis_index("core"), t_place]).astype(jnp.int32)
    own_basis = lax.dynamic_slice_in_dim(in_lines(left_basis), t_place, 1, 0)[0]
    own_rows = lax.dynamic_slice_in_dim(right_basis, place * SHARE, SHARE, 0)
    image = jnp.dot(gradient, right_basis, preferred_element_type=jnp.float32)
    thin, packed = image_lines(own_basis, in_lines(image), pack(gradient))
    packed, thin = lax.optimization_barrier((packed, thin))
    parcels = lax.all_to_all(packed, ("z", "y", "core"), 0, 0)
    strip, right_rows, factors, gram = strip_products(
        where, parcels, own_rows, right_scale, gather_rest(thin)
    )
    other = swap(away_sums(strip, factors))
    sums = home_sums(where, strip, factors, other, gram, swap(gram))
    sums = lax.all_to_all(sums, ("z", "y", "tensor"), 0, 0)
    rows, lines = own_lines(sums, own_basis, left_scale)
    mine, other, _ = gather_sets(lines)
    left_mine, left_gram, right_part = own_side(mine)
    left_other, right_coeff, left_inv, right_inv, left_scale_new, right_scale_new = factor_grams(
        where, left_gram, right_part, other, rows
    )
    left_scale_new, right_scale_new = left_scale_new[0], right_scale_new[0]
    left_damp = (left_scale_new + 1.0) ** (-0.5) - 1.0
    left_mine = times_inverse(left_mine.astype(jnp.float32), left_inv).astype(jnp.bfloat16)
    left_other = times_inverse(left_other.astype(jnp.float32), left_inv).astype(jnp.bfloat16)
    right_new = times_inverse(right_rows, right_inv)
    mine, other, (left_mine, left_other, right_new) = gather_sets(
        right_coeff, (left_mine, left_other, right_new)
    )
    mixed, work = own_mixed(strip, mine, left_mine, right_new)
    update = update_parcels(
        where, strip, other, mixed, work, left_mine, left_other, right_new, left_damp
    )
    left_new = times_inverse(rows[:OWN, :RANK], left_inv)
    left_new, update = lax.optimization_barrier((left_new, update))
    left_new = lax.all_gather(left_new, "tensor", axis=0, tiled=True)
    update = unpack(lax.all_to_all(update, ("z", "y", "core"), 0, 0))
    return (update, left_new, left_scale_new, right_new[None], right_scale_new)


def solution(mesh):
    rows = ("z", "y", "core")
    mesh = jax.sharding.Mesh(mesh.devices.reshape(4, 4, 2, 4), rows + ("tensor",))
    in_specs = (P(rows, "tensor"), P(rows, None), P("tensor", None), P(), P())
    out_specs = (P(rows, "tensor"), P(rows, None), P(), P("tensor", rows, None), P())
    return jax.shard_map(shards, mesh=mesh, in_specs=in_specs, out_specs=out_specs, check_vma=False)
```
